256 devices in a mesh: grp: 4 (over y), ep: 64 (over x, z, core).
Axes of the slice: x: 4, y: 4, z: 8, core: 2. Of those that a mesh axis runs over, the one named last changes fastest.
Arguments:
- layer_input: bfloat16 [65536, 8192], P(('grp', 'ep')), may hold values from -6 to 6
- output_grad: bfloat16 [65536, 8192], P(('grp', 'ep')), may hold values from -0.119628906 to 0.119628906
- adapter_ids: int32 [65536, 1], P(('grp', 'ep')), may hold values from 0 to 63; in each aligned block of 256 rows (0 to 255, 256 to 511, ...) at most 8 rows name the same one
- owner_map: int32 [64], replicated, may hold values from 0 to 63, each once
- weights: bfloat16 [64, 2, 64, 8192], P('ep', None, None, 'grp'), may hold values from -0.0625 to 0.0625
- moment: float32 [64, 2, 64, 8192], P('ep', None, None, 'grp'), may hold values from -1.8 to 1.8
- second: float32 [64, 2, 64, 8192], P('ep', None, None, 'grp'), may hold values from 0.0002 to 0.004
Outputs:
- moment_next: float32 [64, 2, 64, 8192], P('ep', None, None, 'grp')
- second_next: float32 [64, 2, 64, 8192], P('ep', None, None, 'grp')
- direction: float32 [64, 2, 64, 8192], P('ep', None, None, 'grp')
The draws below stay inside these ranges and needn't reach their ends.
Inputs may be any that keep to these rules, and one draw needn't show every extreme that they name: `adapter_ids`: among the rows of one device no adapter appears more than 8 times, and some adapter appears exactly 8 times. `owner_map`: each owner index appears once.
All inputs are finite; a program needn't handle non-finite values.
Results may differ from the reference program's by a relative error of at most 0.0026.
Values may be sent and summed in bfloat16 or wider, within the bound.
A program may use at most 128 MiB of HBM per device.

```python
import math
import jax
import jax.numpy as jnp
import numpy as np
from jax import lax

D = 8192
R = 64
TOK_DEV = 256
STEP = 100
CAP = 8
ADAPTERS = 64
TOKENS = 65536
N_GRP = 4
N_EP = 64


def shard_levels(key, shape, cuts, smallest, largest):
    loudness, own = 1.0, jax.random.fold_in(key, 6)
    for dim, parts in cuts:
        steps = jnp.exp(jax.random.uniform(jax.random.fold_in(own, dim), (parts,), jnp.float32, smallest / len(cuts), largest / len(cuts)))
        loudness = loudness * jnp.repeat(steps, shape[dim] // parts).reshape([-1 if axis == dim else 1 for axis in range(len(shape))])
    return loudness


def assign_block(key, own, number, rows, amount, top, limit, skew):
    sequence = jax.random.permutation(key, amount)
    heavy_load, usual = load_shares(amount, rows * top, limit, skew, True), load_shares(amount, rows * top, limit, skew, False)
    places = jnp.arange(amount)

    def named(tallies, rotation):
        used = int((tallies > 0).sum())
        fixed = max(1, used // 4)
        shifted = fixed + (places - fixed + rotation * (used - fixed)) % max(1, amount - fixed)
        return jnp.zeros((amount,), jnp.int32).at[sequence[jnp.where(places < fixed, places, shifted)]].set(jnp.asarray(tallies, jnp.int32))

    tallies = jnp.where(number % 4 == 0, named(heavy_load, number // 4), named(usual, number - number // 4 - 1))
    mixed = jax.random.permutation(jax.random.fold_in(own, 3), amount)
    source_of, taker = mixed[0:amount // 2 * 2:2], mixed[1:amount // 2 * 2:2]
    room = jnp.minimum(tallies[source_of] - 1, limit - tallies[taker]) // 2
    room = jnp.where((source_of == sequence[0]) | (taker == sequence[0]) | (tallies[taker] == 0), 0, jnp.maximum(room, 0))
    shifted = jax.random.randint(jax.random.fold_in(own, 4), (amount // 2,), 0, 1 << 20) % (room + 1)
    tallies = tallies.at[source_of].add(-shifted).at[taker].add(shifted)
    labels = jnp.searchsorted(jnp.cumsum(tallies), jnp.arange(rows * top), side="right").astype(jnp.int32)
    grid = labels.reshape(top, rows).T
    grid = grid[jax.random.permutation(jax.random.fold_in(own, 1), rows)]
    rotation = jax.random.randint(jax.random.fold_in(own, 2), (rows, 1), 0, top)
    return jnp.take_along_axis(grid, (jnp.arange(top)[None, :] + rotation) % top, axis=1)


def load_shares(count, total, bound, lean, full):
    weights = [(1 << 20) // math.isqrt(rank ** lean) + 1 for rank in range(1, count + 1)]
    largest = bound if full else min(bound, max(-(-total // count), total * weights[0] // sum(weights)))
    least = 1 if total - largest >= count - 1 else 0
    holding, spare = [largest] + [least] * (count - 1), total - largest - least * (count - 1)
    while spare > 0:
        movable = [i for i in range(1, count) if holding[i] < largest] or [i for i in range(1, count) if holding[i] < bound]
        pool, remaining = sum([weights[i] for i in movable]), spare
        for i in movable:
            more = min(bound - holding[i], max(1, remaining * weights[i] // pool), spare)
            holding[i] = holding[i] + more
            spare = spare - more
    return np.array(holding)


def centred(rng, shape, width, reach, cuts=(), held_as=jnp.bfloat16):
    values = width * jax.random.normal(rng, shape, jnp.float32)
    if cuts:
        values = values * shard_levels(rng, shape, cuts, -0.22, 0.18)
    return jnp.clip(values, -reach, reach).astype(held_as)


def setup_inputs(seed: int = 0) -> dict:
    key_list = jax.random.split(jax.random.key(seed), 8)
    layer_input = centred(key_list[0], (TOKENS, D), 1.0, 6.0, ((0, 256),))
    output_grad = centred(key_list[1], (TOKENS, D), 0.02, 0.119628906, ((0, 256),))
    adapter_ids_keys = jax.random.split(jax.random.fold_in(key_list[2], 1), TOKENS // TOK_DEV)
    adapter_ids_turns = jax.random.permutation(jax.random.fold_in(key_list[2], 3), TOKENS // TOK_DEV)
    adapter_ids = jax.vmap(lambda own, number: assign_block(jax.random.fold_in(key_list[2], 2), own, number, TOK_DEV, ADAPTERS, 1, CAP, 2))(adapter_ids_keys, adapter_ids_turns).reshape((TOKENS, 1))
    owner_map = jax.random.permutation(key_list[3], ADAPTERS).astype(jnp.int32)
    weights = centred(key_list[4], (ADAPTERS, 2, R, D), D ** -0.5, 0.0625, ((0, 64), (3, 4)))
    moment = centred(key_list[5], (ADAPTERS, 2, R, D), 0.3, 1.8, ((0, 64), (3, 4)), jnp.float32)
    second = jnp.clip(jnp.exp(math.log(0.004) - 2.9957323 * jax.random.uniform(key_list[6], (ADAPTERS, 2, R, D), jnp.float32) ** shard_levels(key_list[6], (ADAPTERS, 2, R, D), ((0, 64), (3, 4)), -0.2, 0.2)), 0.0002, 0.004)
    return {"layer_input": layer_input, "output_grad": output_grad, "adapter_ids": adapter_ids, "owner_map": owner_map, "weights": weights, "moment": moment, "second": second}


ADAPTER_SCALING = 2.0
BETA_FIRST = 0.9
BETA_SECOND = 0.999
ADAM_EPSILON = 1e-08

def reference(layer_input, output_grad, adapter_ids, owner_map, weights, moment, second):
    total_rows = layer_input.shape[0]
    owner_total = ADAPTERS
    most_rows = N_GRP * N_EP * CAP
    owner_of = owner_map[adapter_ids[:, 0]].astype(jnp.int32)
    owner_hot = (owner_of[:, None] == jnp.arange(owner_total, dtype=jnp.int32)[None, :]).astype(jnp.int32)
    position = lax.optimization_barrier(jnp.sum((jnp.cumsum(owner_hot, axis=0) - 1) * owner_hot, axis=1)).astype(jnp.int32)
    slot_index = (owner_of * most_rows + position).astype(jnp.int32)
    table = jnp.full((owner_total * most_rows,), total_rows, jnp.int32)
    table = table.at[slot_index].set(jnp.arange(total_rows, dtype=jnp.int32)).reshape(owner_total, most_rows)
    padded_input = jnp.concatenate([layer_input, jnp.zeros((1, D), layer_input.dtype)], axis=0)
    padded_grad = jnp.concatenate([output_grad, jnp.zeros((1, D), output_grad.dtype)], axis=0)

    def per_owner(packed):
        index_row, weight_pair = packed
        input_rows = padded_input[index_row]
        incoming_gradients = padded_grad[index_row]
        reduced_input = jnp.dot(input_rows, weight_pair[0].T, preferred_element_type=jnp.float32).astype(jnp.bfloat16)
        reduced_gradient = jnp.dot(incoming_gradients, weight_pair[1].T, preferred_element_type=jnp.float32).astype(jnp.bfloat16)
        down_gradient = ADAPTER_SCALING * jnp.dot(reduced_gradient.T, input_rows, preferred_element_type=jnp.float32)
        up_gradient = ADAPTER_SCALING * jnp.dot(reduced_input.T, incoming_gradients, preferred_element_type=jnp.float32)
        return jnp.stack([down_gradient, up_gradient])
    grads = lax.map(per_owner, (table, weights))
    moment_next = BETA_FIRST * moment + (1.0 - BETA_FIRST) * grads
    second_next = BETA_SECOND * second + (1.0 - BETA_SECOND) * grads * grads
    first_fix = 1.0 - BETA_FIRST ** STEP
    second_fix = 1.0 - BETA_SECOND ** STEP
    direction = moment_next / first_fix / (jnp.sqrt(second_next / second_fix) + ADAM_EPSILON)
    return (moment_next, second_next, direction)
```

```python
import jax
import jax.numpy as jnp
import numpy as np
from jax import lax
from jax.experimental import pallas as pl
from jax.experimental.pallas import tpu as pltpu
from jax.sharding import Mesh, PartitionSpec as P

STEP = 100
CAP = 8
NY, NX, NZ, NC = 4, 4, 8, 2
PEERS = NY * NX * NC
CHIPS = NY * NX
MATES = NX * NC
OWNERS = NX * NZ * NC
HALF = OWNERS // 2
ROWS = 256
RANK = 64
SLICE = 256
UP, DOWN = NZ // 2, NZ // 2 - 1

ADAPTER_SCALING = 2.0
BETA_FIRST = 0.9
BETA_SECOND = 0.999
ADAM_EPSILON = 1e-08

MESH = pl.DeviceIdType.MESH
BF16, F32 = jnp.bfloat16, jnp.float32
NT = (((1,), (1,)), ((), ()))


def adam_step(grads, moment, second):
    moment_next = BETA_FIRST * moment + (1.0 - BETA_FIRST) * grads
    second_next = BETA_SECOND * second + (1.0 - BETA_SECOND) * grads * grads
    first_fix = 1.0 - BETA_FIRST**STEP
    second_fix = 1.0 - BETA_SECOND**STEP
    direction = moment_next / first_fix / (jnp.sqrt(second_next / second_fix) + ADAM_EPSILON)
    return (moment_next, second_next, direction)


def slot_of_rows(adapter_ids, owner_map):
    hot = adapter_ids == jnp.arange(owner_map.shape[0], dtype=jnp.int32)[None, :]
    owner = jnp.sum(jnp.where(hot, owner_map[None, :], 0), axis=1)
    t = jnp.arange(adapter_ids.shape[0], dtype=jnp.int32)
    earlier = (owner[:, None] == owner[None, :]) & (t[:, None] < t[None, :])
    position = jnp.sum(earlier.astype(jnp.int32), axis=0)
    c = owner % NC
    z = (owner // NC) % NZ
    x = owner // (NC * NZ)
    return ((z * NX + x) * NC + c) * CAP + position


def loop(lo, hi, body):
    def step(i, carry):
        body(i)
        return carry

    lax.fori_loop(lo, hi, step, 0)


def kernel(
    x_ref, g_ref, slot_ref, w_ref, out_ref,
    slots, wbuf, recv, spread, packed, part, pair, rsum, own, full, low, ring, last,
    slot_s, slot_r, wx_s, wx_r, wz_s, wz_r, tok_s, tok_r, lc_s, lc_r, lr_s, lr_r, lg_s, lg_r,
    gz_s, gz_r, gx_s, gx_r, here,
):
    y, x, z, c = (lax.axis_index(a) for a in ("y", "x", "z", "c"))
    mate = x * NC + c

    def peer(k, sign=1):
        dy, dx, dc = k // (NX * NC), (k // NC) % NX, k % NC
        return ((y + sign * dy + NY) % NY, (x + sign * dx + NX) % NX, z, (c + dc) % NC)

    def chip(m, sign=1):
        return ((y + sign * (m // NX) + NY) % NY, (x + sign * (m % NX) + NX) % NX, z, c)

    def mate_at(m):
        return (y, (x + m // NC) % NX, z, (c + m % NC) % NC)

    def along(step):
        return (y, x, (z + step + NZ) % NZ, c)

    sibling = (y, x, z, 1 - c)

    def remote(src, dst, send, arrive, device):
        return pltpu.make_async_remote_copy(
            src_ref=src, dst_ref=dst, send_sem=send, recv_sem=arrive,
            device_id=device, device_id_type=MESH,
        )

    def columns(i):
        return pl.ds(pl.multiple_of(i * SLICE, SLICE), SLICE)

    def slot_copy(k):
        return remote(slots.at[0], slots.at[k], slot_s.at[k], slot_r.at[k], peer(k))

    def weight_copy(m):
        d = mate_at(m)
        return remote(
            w_ref.at[:, :, columns(d[1] * NC + d[3])], wbuf.at[z * MATES + mate],
            wx_s.at[m], wx_r.at[m], d,
        )

    def weight_hop(arm, s):
        sign = 1 - 2 * arm
        chunk = wbuf.at[pl.ds((z - sign * s + NZ) % NZ * MATES, MATES)]
        return remote(chunk, chunk, wz_s.at[arm, s], wz_r.at[arm, s], along(sign))

    def weight_wait(arm, s):
        chunk = wbuf.at[pl.ds((z - (1 - 2 * arm) * (s + 1) + NZ) % NZ * MATES, MATES)]
        remote(chunk, chunk, wz_s.at[arm, s], wz_r.at[arm, s], along(1 - 2 * arm)).wait_recv()

    def token_copy(t, k):
        d = peer(k)
        return remote(
            (x_ref, g_ref)[t].at[:, columns((d[0] * NX + d[1]) * NC + d[3])],
            recv.at[t, k], tok_s.at[t, k], tok_r.at[t, k], d,
        )

    def pair_copy(t, m):
        return remote(part.at[2 * m + 1], pair.at[t, m], lc_s.at[t, m], lc_r.at[t, m], sibling)

    def sum_copy(t, m):
        return remote(pair.at[t, m], rsum.at[t, m], lr_s.at[t, m], lr_r.at[t, m], chip(m, -1))

    def low_copy(t, k):
        return remote(own.at[t], full.at[t, k], lg_s.at[t, k], lg_r.at[t, k], peer(k))

    def ring_copy(t, arm, s):
        sign = (1 - 2 * arm) * (1 - 2 * t)
        return remote(
            ring.at[t, arm * (UP + 1) + s], ring.at[t, arm * (UP + 1) + s + 1],
            gz_s.at[t, arm * UP + s], gz_r.at[t, arm * UP + s], along(-sign),
        )

    def grad_copy(t, m):
        d = mate_at(m)
        return remote(
            last.at[t, d[1] * NC + d[3]], out_ref.at[1 - t, :, columns(mate)],
            gx_s.at[t, m], gx_r.at[t, m], d,
        )

    def hot(k, half):
        rows = lax.broadcasted_iota(jnp.int32, (HALF * CAP, ROWS), 0) + half * (HALF * CAP)
        return jnp.where(rows == slots[k], 1.0, 0.0).astype(BF16)

    barrier = pltpu.get_barrier_semaphore()

    def greet(k):
        pl.semaphore_signal(barrier, inc=1, device_id=peer(k), device_id_type=MESH)

    slots[0] = slot_ref[...]
    loop(1, PEERS, greet)
    for step in (1, -1):
        pl.semaphore_signal(barrier, inc=1, device_id=along(step), device_id_type=MESH)
    pl.semaphore_wait(barrier, PEERS + 1)

    loop(1, MATES, lambda m: weight_copy(m).start())
    loop(1, PEERS, lambda k: slot_copy(k).start())

    def order(i):
        return (i * (13 + 6 * c)) % PEERS

    for t in range(2):
        loop(1, PEERS, lambda i: token_copy(t, order(i)).start())
    mine = [
        pltpu.make_async_copy(w_ref.at[:, :, columns(mate)], wbuf.at[z * MATES + mate], here.at[0])
    ] + [
        pltpu.make_async_copy(
            (x_ref, g_ref)[t].at[:, columns(y * MATES + mate)], recv.at[t, 0], here.at[1 + t]
        )
        for t in range(2)
    ]
    for copy in mine:
        copy.start()
    for copy in mine:
        copy.wait()

    loop(1, MATES, lambda m: weight_copy(m).wait_recv())
    weight_hop(0, 0).start()
    weight_hop(1, 0).start()
    loop(1, PEERS, lambda k: slot_copy(k).wait_recv())

    def spread_rows(t, j):
        halves = []
        for half in range(2):
            both = [
                jnp.dot(hot(2 * j + i, half), recv[t, 2 * j + i], preferred_element_type=F32)
                .reshape(HALF, CAP, SLICE)
                for i in range(2)
            ]
            halves.append(jnp.concatenate(both, axis=1).astype(BF16))
        at = pl.ds(pl.multiple_of(2 * CAP * j, 2 * CAP), 2 * CAP)
        spread[t, 0:HALF, at, :] = halves[0]
        spread[t, HALF:OWNERS, at, :] = halves[1]

    def take_rows(t, j):
        @pl.when(j > 0)
        def _():
            token_copy(t, 2 * j).wait_recv()

        token_copy(t, 2 * j + 1).wait_recv()
        spread_rows(t, j)

    def low_parts(t, p):
        packed[p] = jnp.concatenate(
            [
                lax.dot_general(spread[t, o], wbuf[o, t], NT, preferred_element_type=F32)
                for o in (p, p + HALF)
            ],
            axis=1,
        )

    def to_rows(k):
        lanes = packed[:, pl.ds(pl.multiple_of(CAP * k, CAP), CAP), :].reshape(HALF * CAP, 2 * RANK).T
        high = lanes.astype(BF16)
        rest = (lanes - high.astype(F32)).astype(BF16)
        total = jnp.zeros((2 * RANK, ROWS), F32)
        for half in range(2):
            r = slice(half * RANK, (half + 1) * RANK)
            total += jnp.dot(
                jnp.concatenate([high[r], rest[r]], axis=0), hot(k, half), preferred_element_type=F32
            )
        part[k] = total[:RANK] + total[RANK:]

    def low_send(t):
        loop(0, HALF, lambda p: low_parts(t, p))

        def both(m):
            to_rows(2 * m + 1)
            pair_copy(t, m).start()
            to_rows(2 * m)

        loop(0, CHIPS, both)

    def low_sum(t):
        def over_pair(m):
            pair_copy(t, m).wait_recv()
            pair[t, m] = pair[t, m] + part[2 * m]

            @pl.when(m > 0)
            def _():
                sum_copy(t, m).start()

        loop(0, CHIPS, over_pair)
        loop(1, CHIPS, lambda m: sum_copy(t, m).wait_recv())
        total = pair[t, 0]
        for m in range(1, CHIPS):
            total += rsum[t, m]
        own[t] = total.astype(BF16)
        full[t, 0] = total.astype(BF16)
        loop(1, PEERS, lambda k: low_copy(t, k).start())

    def low_spread(t):
        loop(1, PEERS, lambda k: low_copy(t, k).wait_recv())

        def two(j):
            both = []
            for i in range(2):
                k = 2 * j + i
                both.append(
                    jnp.concatenate(
                        [
                            lax.dot_general(hot(k, half), full[t, k], NT, preferred_element_type=F32)
                            for half in range(2)
                        ],
                        axis=1,
                    ).reshape(HALF, CAP, 2 * RANK)
                )
            at = pl.ds(pl.multiple_of(2 * CAP * j, 2 * CAP), 2 * CAP)
            low[t, :, at, :] = jnp.concatenate(both, axis=1).astype(BF16)

        loop(0, PEERS // 2, two)

    def outer(t, plane, store):
        def one(i):
            o = plane * MATES + i
            p, half = o % HALF, o // HALF
            lhs = low[t, p].T.astype(BF16)
            lhs = jnp.where(half == 0, lhs[:RANK], lhs[RANK:])
            store(i, jnp.dot(lhs, spread[1 - t, o], preferred_element_type=F32))

        loop(0, MATES, one)

    def ring_step(t, arm, s):
        sign = (1 - 2 * arm) * (1 - 2 * t)
        hops = (UP, DOWN)[arm]
        place = arm * (UP + 1) + s
        if s > 0:
            ring_copy(t, arm, s - 1).wait_recv()

        def store(i, term):
            ring[t, place, i] = term if s == 0 else ring[t, place, i] + term

        outer(t, (z - sign * (hops - s) + NZ) % NZ, store)
        ring_copy(t, arm, s).start()

    def ring_end(t):
        ring_copy(t, 0, UP - 1).wait_recv()
        ring_copy(t, 1, DOWN - 1).wait_recv()

        def store(i, term):
            last[t, i] = term + ring[t, UP, i] + ring[t, UP + 1 + DOWN, i]

        outer(t, z, store)
        loop(1, MATES, lambda m: grad_copy(t, m).start())
        out_ref[1 - t, :, columns(mate)] = last[t, mate]

    def ring_both(t, s):
        ring_step(t, 0, s)
        if s < DOWN:
            ring_step(t, 1, s)

    for s in range(1, UP + 1):
        loop(4 * (s - 1), 4 * s, lambda j: take_rows(0, j))
        weight_wait(0, s - 1)
        if s < UP:
            weight_hop(0, s).start()
            weight_wait(1, s - 1)
        if s < DOWN:
            weight_hop(1, s).start()
    low_send(0)
    low_sum(0)
    loop(0, PEERS // 2, lambda j: take_rows(1, j))
    loop(0, CHIPS, lambda m: pair_copy(0, m).wait_send())
    low_send(1)
    low_spread(0)
    ring_both(0, 0)
    low_sum(1)
    ring_both(0, 1)
    low_spread(1)
    ring_both(1, 0)
    ring_both(0, 2)
    ring_both(1, 1)
    ring_both(0, 3)
    ring_both(1, 2)
    ring_end(0)
    ring_both(1, 3)
    ring_end(1)

    for t in range(2):
        loop(1, MATES, lambda m: grad_copy(t, m).wait())
        for arm, hops in enumerate((UP, DOWN)):
            for s in range(hops):
                ring_copy(t, arm, s).wait_send()
        loop(1, PEERS, lambda k: low_copy(t, k).wait_send())
        loop(1, CHIPS, lambda m: sum_copy(t, m).wait_send())
        loop(1, PEERS, lambda k: token_copy(t, k).wait_send())
    loop(0, CHIPS, lambda m: pair_copy(1, m).wait_send())
    loop(1, PEERS, lambda k: slot_copy(k).wait_send())
    loop(1, MATES, lambda m: weight_copy(m).wait_send())
    for arm, hops in enumerate((UP, DOWN)):
        for s in range(hops):
            weight_hop(arm, s).wait_send()


def summed_grads(layer_input, output_grad, slot, weights):
    vmem = pl.BlockSpec(memory_space=pltpu.VMEM)
    hbm = pl.BlockSpec(memory_space=pl.ANY)
    sems = [
        (PEERS,), (PEERS,), (MATES,), (MATES,), (2, UP), (2, UP), (2, PEERS), (2, PEERS),
        (2, CHIPS), (2, CHIPS), (2, CHIPS), (2, CHIPS), (2, PEERS), (2, PEERS),
        (2, UP + DOWN), (2, UP + DOWN), (2, MATES), (2, MATES), (3,),
    ]
    return pl.pallas_call(
        kernel,
        out_shape=jax.ShapeDtypeStruct((2, RANK, MATES * SLICE), F32),
        in_specs=[hbm, hbm, vmem, vmem],
        out_specs=vmem,
        scratch_shapes=[
            pltpu.VMEM((PEERS, 1, ROWS), jnp.int32),
            pltpu.VMEM((OWNERS, 2, RANK, SLICE), BF16),
            pltpu.VMEM((2, PEERS, ROWS, SLICE), BF16),
            pltpu.VMEM((2, OWNERS, PEERS * CAP, SLICE), BF16),
            pltpu.VMEM((HALF, PEERS * CAP, 2 * RANK), F32),
            pltpu.VMEM((PEERS, RANK, ROWS), F32),
            pltpu.VMEM((2, CHIPS, RANK, ROWS), F32),
            pltpu.VMEM((2, CHIPS, RANK, ROWS), F32),
            pltpu.VMEM((2, RANK, ROWS), BF16),
            pltpu.VMEM((2, PEERS, RANK, ROWS), BF16),
            pltpu.VMEM((2, HALF, PEERS * CAP, 2 * RANK), BF16),
            pltpu.VMEM((2, UP + DOWN + 2, MATES, RANK, SLICE), F32),
            pltpu.VMEM((2, MATES, RANK, SLICE), F32),
            *[pltpu.SemaphoreType.DMA(s) for s in sems],
        ],
        compiler_params=pltpu.CompilerParams(
            collective_id=0, has_side_effects=True, vmem_limit_bytes=62 << 20
        ),
        cost_estimate=pl.CostEstimate(flops=20 << 30, bytes_accessed=16 << 20, transcendentals=0),
    )(layer_input, output_grad, slot, weights)


def per_device(layer_input, output_grad, adapter_ids, owner_map, weights, moment, second):
    slot = slot_of_rows(adapter_ids, owner_map)[None, :]
    grads = ADAPTER_SCALING * summed_grads(layer_input, output_grad, slot, weights[0])
    return adam_step(grads[None], moment, second)


def solution(mesh):
    split = Mesh(np.asarray(mesh.devices).reshape(NY, NX, NZ, NC), ("y", "x", "z", "c"))
    ep = ("x", "z", "c")
    tokens = P(("y",) + ep, None)
    state = P(ep, None, None, "y")
    return jax.shard_map(
        per_device,
        mesh=split,
        in_specs=(tokens, tokens, tokens, P(), state, state, state),
        out_specs=(state, state, state),
        check_vma=False,
    )
```

```python
import jax
import jax.numpy as jnp
import numpy as np
from jax import lax
from jax.experimental import pallas as pl
from jax.experimental.pallas import tpu as pltpu
from jax.sharding import Mesh, PartitionSpec as P

STEP = 100
CAP = 8
NY, NX, NZ, NC = 4, 4, 8, 2
PEERS = NY * NX * NC
CHIPS = NY * NX
MATES = NX * NC
OWNERS = NX * NZ * NC
HALF = OWNERS // 2
ROWS = 256
RANK = 64
SLICE = 256
QUARTER = MATES // 2
UP, DOWN = NZ // 2, NZ // 2 - 1

ADAPTER_SCALING = 2.0
BETA_FIRST = 0.9
BETA_SECOND = 0.999
ADAM_EPSILON = 1e-08

MESH = pl.DeviceIdType.MESH
BF16, F32 = jnp.bfloat16, jnp.float32
NT = (((1,), (1,)), ((), ()))


def adam_step(grads, moment, second):
    moment_next = BETA_FIRST * moment + (1.0 - BETA_FIRST) * grads
    second_next = BETA_SECOND * second + (1.0 - BETA_SECOND) * grads * grads
    first_fix = 1.0 - BETA_FIRST**STEP
    second_fix = 1.0 - BETA_SECOND**STEP
    direction = moment_next / first_fix / (jnp.sqrt(second_next / second_fix) + ADAM_EPSILON)
    return (moment_next, second_next, direction)


def slot_of_rows(adapter_ids, owner_map):
    hot = adapter_ids == jnp.arange(owner_map.shape[0], dtype=jnp.int32)[None, :]
    owner = jnp.sum(jnp.where(hot, owner_map[None, :], 0), axis=1)
    t = jnp.arange(adapter_ids.shape[0], dtype=jnp.int32)
    earlier = (owner[:, None] == owner[None, :]) & (t[:, None] < t[None, :])
    position = jnp.sum(earlier.astype(jnp.int32), axis=0)
    c = owner % NC
    z = (owner // NC) % NZ
    x = owner // (NC * NZ)
    return ((z * NX + x) * NC + c) * CAP + position


def loop(lo, hi, body):
    def step(i, carry):
        body(i)
        return carry

    lax.fori_loop(lo, hi, step, 0)


def kernel(
    x_ref, g_ref, slot_ref, w_ref, out_ref,
    slots, wbuf, recv, spread, packed, part, pair, rsum, full, low, first, ring, last,
    slot_s, slot_r, wx_s, wx_r, wz_s, wz_r, tok_s, tok_r, lc_s, lc_r, lr_s, lr_r, lg_s, lg_r, lf_s, lf_r,
    gz_s, gz_r, gx_s, gx_r, here,
):
    y, x, z, c = (lax.axis_index(a) for a in ("y", "x", "z", "c"))
    mate = x * NC + c

    def peer(k, sign=1):
        dy, dx, dc = k // (NX * NC), (k // NC) % NX, k % NC
        return ((y + sign * dy + NY) % NY, (x + sign * dx + NX) % NX, z, (c + dc) % NC)

    def chip(m, sign=1):
        return ((y + sign * (m // NX) + NY) % NY, (x + sign * (m % NX) + NX) % NX, z, c)

    def mate_at(m):
        return (y, (x + m // NC) % NX, z, (c + m % NC) % NC)

    def along(step):
        return (y, x, (z + step + NZ) % NZ, c)

    sibling = (y, x, z, 1 - c)

    def remote(src, dst, send, arrive, device):
        return pltpu.make_async_remote_copy(
            src_ref=src, dst_ref=dst, send_sem=send, recv_sem=arrive,
            device_id=device, device_id_type=MESH,
        )

    def columns(i):
        return pl.ds(pl.multiple_of(i * SLICE, SLICE), SLICE)

    def slot_copy(k):
        return remote(slots.at[0], slots.at[k], slot_s.at[k], slot_r.at[k], peer(k))

    def weight_copy(m):
        d = mate_at(m)
        return remote(
            w_ref.at[:, :, columns(d[1] * NC + d[3])], wbuf.at[z * MATES + mate],
            wx_s.at[m], wx_r.at[m], d,
        )

    def weight_hop(arm, s):
        sign = 1 - 2 * arm
        chunk = wbuf.at[pl.ds((z - sign * s + NZ) % NZ * MATES, MATES)]
        return remote(chunk, chunk, wz_s.at[arm, s], wz_r.at[arm, s], along(sign))

    def weight_wait(arm, s):
        chunk = wbuf.at[pl.ds((z - (1 - 2 * arm) * (s + 1) + NZ) % NZ * MATES, MATES)]
        remote(chunk, chunk, wz_s.at[arm, s], wz_r.at[arm, s], along(1 - 2 * arm)).wait_recv()

    def token_copy(t, k):
        d = peer(k)
        return remote(
            (x_ref, g_ref)[t].at[:, columns((d[0] * NX + d[1]) * NC + d[3])],
            recv.at[t, k], tok_s.at[t, k], tok_r.at[t, k], d,
        )

    def pair_copy(t, m):
        return remote(part.at[2 * m + 1], pair.at[t, m], lc_s.at[t, m], lc_r.at[t, m], sibling)

    def sum_copy(t, m):
        return remote(pair.at[t, m], rsum.at[t, m], lr_s.at[t, m], lr_r.at[t, m], chip(m, -1))

    def low_copy(t, m):
        return remote(
            full.at[t, 0], full.at[t, 2 * m], lg_s.at[t, m], lg_r.at[t, m], chip(m)
        )

    def low_pass(t, m):
        return remote(
            full.at[t, 2 * m], full.at[t, 2 * m + 1], lf_s.at[t, m], lf_r.at[t, m], sibling
        )

    def ring_copy(t, h, arm, s):
        sign = (1 - 2 * arm) * (1 - 2 * h)
        sem = arm * UP + s
        src, dst = (
            (ring.at[t, h, sem - 1], ring.at[t, h, sem])
            if s
            else (first.at[t, h, arm, 0], first.at[t, h, arm, 1])
        )
        return remote(src, dst, gz_s.at[t, h, sem], gz_r.at[t, h, sem], along(-sign))

    def grad_copy(t, m):
        d = mate_at(m)
        return remote(
            last.at[t, d[1] * NC + d[3]], out_ref.at[1 - t, :, columns(mate)],
            gx_s.at[t, m], gx_r.at[t, m], d,
        )

    def hot(k, half):
        rows = lax.broadcasted_iota(jnp.int32, (HALF * CAP, ROWS), 0) + half * (HALF * CAP)
        return jnp.where(rows == slots[k], 1.0, 0.0).astype(BF16)

    barrier = pltpu.get_barrier_semaphore()

    def greet(k):
        pl.semaphore_signal(barrier, inc=1, device_id=peer(k), device_id_type=MESH)

    slots[0] = slot_ref[...]
    loop(1, PEERS, greet)
    for step in (1, -1):
        pl.semaphore_signal(barrier, inc=1, device_id=along(step), device_id_type=MESH)
    pl.semaphore_wait(barrier, PEERS + 1)

    loop(1, MATES, lambda m: weight_copy(m).start())
    loop(1, PEERS, lambda k: slot_copy(k).start())

    def chip_at(core, i):
        return (i * (7 + 2 * core)) % CHIPS

    def send_rows(t, lo, hi):
        def both(i):
            m = chip_at(c, i)

            @pl.when(m > 0)
            def _():
                token_copy(t, 2 * m).start()

            token_copy(t, 2 * m + 1).start()

        loop(lo, hi, both)

    def pair_at(i):
        return 2 * chip_at(c, i), 2 * chip_at(1 - c, i) + 1

    send_rows(0, 0, CHIPS)
    send_rows(1, 0, CHIPS)
    mine = [
        pltpu.make_async_copy(w_ref.at[:, :, columns(mate)], wbuf.at[z * MATES + mate], here.at[0])
    ] + [
        pltpu.make_async_copy(
            (x_ref, g_ref)[t].at[:, columns(y * MATES + mate)], recv.at[t, 0], here.at[1 + t]
        )
        for t in range(2)
    ]
    for copy in mine:
        copy.start()
    for copy in mine:
        copy.wait()

    loop(1, MATES, lambda m: weight_copy(m).wait_recv())
    weight_hop(0, 0).start()
    weight_hop(1, 0).start()
    loop(1, PEERS, lambda k: slot_copy(k).wait_recv())

    def rows_of(i):
        return pl.ds(pl.multiple_of(2 * CAP * i, 2 * CAP), 2 * CAP)

    def take_rows(t, i):
        ks = pair_at(i)

        @pl.when(i > 0)
        def _():
            token_copy(t, ks[0]).wait_recv()

        token_copy(t, ks[1]).wait_recv()
        for half in range(2):
            both = [
                jnp.dot(hot(k, half), recv[t, k], preferred_element_type=F32)
                .reshape(HALF, CAP, SLICE)
                for k in ks
            ]
            spread[t, half * HALF : (half + 1) * HALF, rows_of(i), :] = jnp.concatenate(
                both, axis=1
            ).astype(BF16)

    def to_rows(k, place):
        at = pl.ds(pl.multiple_of(CAP * place, CAP), CAP)
        lanes = packed[:, at, :].reshape(HALF * CAP, 2 * RANK).T
        high = lanes.astype(BF16)
        rest = (lanes - high.astype(F32)).astype(BF16)
        total = jnp.zeros((2 * RANK, ROWS), F32)
        for half in range(2):
            r = slice(half * RANK, (half + 1) * RANK)
            total += jnp.dot(
                jnp.concatenate([high[r], rest[r]], axis=0), hot(k, half), preferred_element_type=F32
            )
        part[k] = total[:RANK] + total[RANK:]

    def low_send(t, half):
        depth = PEERS * CAP // 2
        rows = slice(half * depth, (half + 1) * depth)

        def low_parts(p):
            packed[p, rows] = jnp.concatenate(
                [
                    lax.dot_general(spread[t, o, rows], wbuf[o, t], NT, preferred_element_type=F32)
                    for o in (p, p + HALF)
                ],
                axis=1,
            )

        def give(i):
            mine, theirs = pair_at(i)
            to_rows(theirs, 2 * i + 1)
            pair_copy(t, chip_at(1 - c, i)).start()
            to_rows(mine, 2 * i)

        def add(i):
            m = chip_at(c, i)
            pair_copy(t, m).wait_recv()
            pair[t, m] = pair[t, m] + part[2 * m]

            @pl.when(m > 0)
            def _():
                sum_copy(t, m).start()

        loop(0, HALF, low_parts)
        steps = half * CHIPS // 2, (half + 1) * CHIPS // 2
        loop(*steps, give)
        loop(*steps, add)

    def low_sum(t):
        loop(1, CHIPS, lambda m: sum_copy(t, m).wait_recv())
        total = pair[t, 0]
        for m in range(1, CHIPS):
            total += rsum[t, m]
        full[t, 0] = total.astype(BF16)
        low_pass(t, 0).start()
        loop(1, CHIPS, lambda i: low_copy(t, chip_at(c, i)).start())

    def low_spread(t):
        def hand_on(i):
            m = chip_at(c, i)
            low_copy(t, m).wait_recv()
            low_pass(t, m).start()

        def two(i):
            low_pass(t, chip_at(1 - c, i)).wait_recv()
            both = [
                jnp.concatenate(
                    [
                        lax.dot_general(hot(k, half), full[t, k], NT, preferred_element_type=F32)
                        for half in range(2)
                    ],
                    axis=1,
                ).reshape(HALF, CAP, 2 * RANK)
                for k in pair_at(i)
            ]
            low[t, :, rows_of(i), :] = jnp.concatenate(both, axis=1).astype(BF16)

        loop(1, CHIPS, hand_on)
        loop(0, CHIPS, two)

    def outer(t, plane, h, store):
        def one(i):
            o = plane * MATES + h * QUARTER + i
            p, half = o % HALF, o // HALF
            lhs = low[t, p].T
            lhs = jnp.where(half == 0, lhs[:RANK], lhs[RANK:])
            store(i, jnp.dot(lhs, spread[1 - t, o], preferred_element_type=F32))

        loop(0, QUARTER, one)

    def ring_step(t, h, arm, s):
        sign = (1 - 2 * arm) * (1 - 2 * h)
        hops = (UP, DOWN)[arm]
        place = arm * UP + s - 1
        if s > 0:
            ring_copy(t, h, arm, s - 1).wait_recv()

        def store(i, term):
            if s == 0:
                first[t, h, arm, 0, i] = term.astype(BF16)
            elif s == 1:
                ring[t, h, place, i] = first[t, h, arm, 1, i].astype(F32) + term
            else:
                ring[t, h, place, i] = ring[t, h, place, i] + term

        outer(t, (z - sign * (hops - s) + NZ) % NZ, h, store)
        ring_copy(t, h, arm, s).start()

    def ring_end(t):
        for h in range(2):
            ring_copy(t, h, 0, UP - 1).wait_recv()
            ring_copy(t, h, 1, DOWN - 1).wait_recv()

            def store(i, term, h=h):
                arrived = ring[t, h, UP - 1, i] + ring[t, h, UP + DOWN - 1, i]
                last[t, h * QUARTER + i] = term + arrived

            outer(t, z, h, store)

            def give(i, h=h):
                j = h * QUARTER + i
                m = (j // NC - x + NX) % NX * NC + (j % NC - c + NC) % NC

                @pl.when(m > 0)
                def _():
                    grad_copy(t, m).start()

            loop(0, QUARTER, give)
        out_ref[1 - t, :, columns(mate)] = last[t, mate]

    def ring_both(t, s):
        for arm in range(2 if s < DOWN else 1):
            for h in range(2):
                ring_step(t, h, arm, s)

    for s in range(1, UP + 1):
        loop(4 * (s - 1), 4 * s, lambda i: take_rows(0, i))
        weight_wait(0, s - 1)
        if s < UP:
            weight_hop(0, s).start()
            weight_wait(1, s - 1)
        if s < DOWN:
            weight_hop(1, s).start()
    low_send(0, 0)
    low_send(0, 1)
    low_sum(0)
    loop(0, CHIPS // 2, lambda i: take_rows(1, i))
    loop(0, CHIPS, lambda m: pair_copy(0, m).wait_send())
    low_send(1, 0)
    low_spread(0)
    loop(CHIPS // 2, CHIPS, lambda i: take_rows(1, i))
    ring_both(0, 0)
    low_send(1, 1)
    ring_both(0, 1)
    low_sum(1)
    ring_both(0, 2)
    low_spread(1)
    ring_both(1, 0)
    ring_both(0, 3)
    ring_both(1, 1)
    ring_end(0)
    ring_both(1, 2)
    ring_both(1, 3)
    ring_end(1)

    for t in range(2):
        loop(1, MATES, lambda m: grad_copy(t, m).wait())
        for arm, hops in enumerate((UP, DOWN)):
            for s in range(hops):
                for h in range(2):
                    ring_copy(t, h, arm, s).wait_send()
        loop(1, CHIPS, lambda m: low_copy(t, m).wait_send())
        loop(0, CHIPS, lambda m: low_pass(t, m).wait_send())
        loop(1, CHIPS, lambda m: sum_copy(t, m).wait_send())
        loop(1, PEERS, lambda k: token_copy(t, k).wait_send())
    loop(0, CHIPS, lambda m: pair_copy(1, m).wait_send())
    loop(1, PEERS, lambda k: slot_copy(k).wait_send())
    loop(1, MATES, lambda m: weight_copy(m).wait_send())
    for arm, hops in enumerate((UP, DOWN)):
        for s in range(hops):
            weight_hop(arm, s).wait_send()


def summed_grads(layer_input, output_grad, slot, weights):
    vmem = pl.BlockSpec(memory_space=pltpu.VMEM)
    hbm = pl.BlockSpec(memory_space=pl.ANY)
    sems = [
        (PEERS,), (PEERS,), (MATES,), (MATES,), (2, UP), (2, UP), (2, PEERS), (2, PEERS),
        (2, CHIPS), (2, CHIPS), (2, CHIPS), (2, CHIPS), (2, CHIPS), (2, CHIPS), (2, CHIPS), (2, CHIPS),
        (2, 2, UP + DOWN), (2, 2, UP + DOWN), (2, MATES), (2, MATES), (3,),
    ]
    return pl.pallas_call(
        kernel,
        out_shape=jax.ShapeDtypeStruct((2, RANK, MATES * SLICE), F32),
        in_specs=[hbm, hbm, vmem, vmem],
        out_specs=vmem,
        scratch_shapes=[
            pltpu.VMEM((PEERS, 1, ROWS), jnp.int32),
            pltpu.VMEM((OWNERS, 2, RANK, SLICE), BF16),
            pltpu.VMEM((2, PEERS, ROWS, SLICE), BF16),
            pltpu.VMEM((2, OWNERS, PEERS * CAP, SLICE), BF16),
            pltpu.VMEM((HALF, PEERS * CAP, 2 * RANK), F32),
            pltpu.VMEM((PEERS, RANK, ROWS), F32),
            pltpu.VMEM((2, CHIPS, RANK, ROWS), F32),
            pltpu.VMEM((2, CHIPS, RANK, ROWS), F32),
            pltpu.VMEM((2, PEERS, RANK, ROWS), BF16),
            pltpu.VMEM((2, HALF, PEERS * CAP, 2 * RANK), BF16),
            pltpu.VMEM((2, 2, 2, 2, QUARTER, RANK, SLICE), BF16),
            pltpu.VMEM((2, 2, UP + DOWN, QUARTER, RANK, SLICE), F32),
            pltpu.VMEM((2, MATES, RANK, SLICE), F32),
            *[pltpu.SemaphoreType.DMA(s) for s in sems],
        ],
        compiler_params=pltpu.CompilerParams(
            collective_id=0, has_side_effects=True, vmem_limit_bytes=62 << 20
        ),
        cost_estimate=pl.CostEstimate(flops=20 << 30, bytes_accessed=16 << 20, transcendentals=0),
    )(layer_input, output_grad, slot, weights)


def per_device(layer_input, output_grad, adapter_ids, owner_map, weights, moment, second):
    slot = slot_of_rows(adapter_ids, owner_map)[None, :]
    grads = ADAPTER_SCALING * summed_grads(layer_input, output_grad, slot, weights[0])
    return adam_step(grads[None], moment, second)


def solution(mesh):
    split = Mesh(np.asarray(mesh.devices).reshape(NY, NX, NZ, NC), ("y", "x", "z", "c"))
    ep = ("x", "z", "c")
    tokens = P(("y",) + ep, None)
    state = P(ep, None, None, "y")
    return jax.shard_map(
        per_device,
        mesh=split,
        in_specs=(tokens, tokens, tokens, P(), state, state, state),
        out_specs=(state, state, state),
        check_vma=False,
    )
```

```python
import jax
import jax.numpy as jnp
import numpy as np
from jax import lax
from jax.experimental import pallas as pl
from jax.experimental.pallas import tpu as pltpu
from jax.sharding import Mesh, PartitionSpec as P

STEP = 100
CAP = 8
NY, NX, NZ, NC = 4, 4, 8, 2
PEERS = NY * NX * NC
CHIPS = NY * NX
MATES = NX * NC
OWNERS = NX * NZ * NC
HALF = OWNERS // 2
ROWS = 256
RANK = 64
SLICE = 256
HOPS = 5, 9, 12
SUM_AT, SPREAD_AT = 5, 12
WINDOW = 8
EXTRA = 3
QUARTER = MATES // 2
UP, DOWN = NZ // 2, NZ // 2 - 1

ADAPTER_SCALING = 2.0
BETA_FIRST = 0.9
BETA_SECOND = 0.999
ADAM_EPSILON = 1e-08

MESH = pl.DeviceIdType.MESH
BF16, F32 = jnp.bfloat16, jnp.float32
NT = (((1,), (1,)), ((), ()))


def adam_step(grads, moment, second):
    moment_next = BETA_FIRST * moment + (1.0 - BETA_FIRST) * grads
    second_next = BETA_SECOND * second + (1.0 - BETA_SECOND) * grads * grads
    first_fix = 1.0 - BETA_FIRST**STEP
    second_fix = 1.0 - BETA_SECOND**STEP
    direction = moment_next / first_fix / (jnp.sqrt(second_next / second_fix) + ADAM_EPSILON)
    return (moment_next, second_next, direction)


def slot_of_rows(adapter_ids, owner_map):
    hot = adapter_ids == jnp.arange(owner_map.shape[0], dtype=jnp.int32)[None, :]
    owner = jnp.sum(jnp.where(hot, owner_map[None, :], 0), axis=1)
    t = jnp.arange(adapter_ids.shape[0], dtype=jnp.int32)
    earlier = (owner[:, None] == owner[None, :]) & (t[:, None] < t[None, :])
    position = jnp.sum(earlier.astype(jnp.int32), axis=0)
    c = owner % NC
    z = (owner // NC) % NZ
    x = owner // (NC * NZ)
    return ((z * NX + x) * NC + c) * CAP + position


def loop(lo, hi, body):
    def step(i, carry):
        body(i)
        return carry

    lax.fori_loop(lo, hi, step, 0)


def kernel(
    x_ref, g_ref, slot_ref, w_ref, out_ref,
    slots, wbuf, recv, spread, packed, part, pair, rsum, full, low, first, ring, last,
    slot_s, slot_r, wx_s, wx_r, wz_s, wz_r, tok_s, tok_r, lc_s, lc_r, lr_s, lr_r, lg_s, lg_r, lf_s, lf_r,
    gz_s, gz_r, gx_s, gx_r, here,
):
    y, x, z, c = (lax.axis_index(a) for a in ("y", "x", "z", "c"))
    mate = x * NC + c

    def peer(k, sign=1):
        dy, dx, dc = k // (NX * NC), (k // NC) % NX, k % NC
        return ((y + sign * dy + NY) % NY, (x + sign * dx + NX) % NX, z, (c + dc) % NC)

    def chip(m, sign=1):
        return ((y + sign * (m // NX) + NY) % NY, (x + sign * (m % NX) + NX) % NX, z, c)

    def mate_at(m):
        return (y, (x + m // NC) % NX, z, (c + m % NC) % NC)

    def along(step):
        return (y, x, (z + step + NZ) % NZ, c)

    sibling = (y, x, z, 1 - c)

    def remote(src, dst, send, arrive, device):
        return pltpu.make_async_remote_copy(
            src_ref=src, dst_ref=dst, send_sem=send, recv_sem=arrive,
            device_id=device, device_id_type=MESH,
        )

    def columns(i):
        return pl.ds(pl.multiple_of(i * SLICE, SLICE), SLICE)

    def slot_copy(k):
        return remote(slots.at[0], slots.at[k], slot_s.at[k], slot_r.at[k], peer(k))

    def weight_copy(m):
        d = mate_at(m)
        return remote(
            w_ref.at[:, :, columns(d[1] * NC + d[3])], wbuf.at[z * MATES + mate],
            wx_s.at[m], wx_r.at[m], d,
        )

    def weight_hop(arm, s):
        sign = 1 - 2 * arm
        chunk = wbuf.at[pl.ds((z - sign * s + NZ) % NZ * MATES, MATES)]
        return remote(chunk, chunk, wz_s.at[arm, s], wz_r.at[arm, s], along(sign))

    def weight_wait(arm, s):
        chunk = wbuf.at[pl.ds((z - (1 - 2 * arm) * (s + 1) + NZ) % NZ * MATES, MATES)]
        remote(chunk, chunk, wz_s.at[arm, s], wz_r.at[arm, s], along(1 - 2 * arm)).wait_recv()

    def token_copy(t, k):
        d = peer(k)
        return remote(
            (x_ref, g_ref)[t].at[:, columns((d[0] * NX + d[1]) * NC + d[3])],
            recv.at[t, k], tok_s.at[t, k], tok_r.at[t, k], d,
        )

    def pair_copy(t, m):
        return remote(part.at[2 * m + 1], pair.at[t, m], lc_s.at[t, m], lc_r.at[t, m], sibling)

    def sum_copy(t, m):
        return remote(pair.at[t, m], rsum.at[t, m], lr_s.at[t, m], lr_r.at[t, m], chip(m, -1))

    def low_copy(t, m):
        return remote(
            full.at[t, 0], full.at[t, 2 * m], lg_s.at[t, m], lg_r.at[t, m], chip(m)
        )

    def low_pass(t, m):
        return remote(
            full.at[t, 2 * m], full.at[t, 2 * m + 1], lf_s.at[t, m], lf_r.at[t, m], sibling
        )

    def ring_copy(t, h, arm, s):
        sign = (1 - 2 * arm) * (1 - 2 * h)
        sem = arm * UP + s
        src, dst = (
            (ring.at[t, h, sem - 1], ring.at[t, h, sem])
            if s
            else (first.at[t, h, arm, 0], first.at[t, h, arm, 1])
        )
        return remote(src, dst, gz_s.at[t, h, sem], gz_r.at[t, h, sem], along(-sign))

    def grad_copy(t, m):
        d = mate_at(m)
        return remote(
            last.at[t, d[1] * NC + d[3]], out_ref.at[1 - t, :, columns(mate)],
            gx_s.at[t, m], gx_r.at[t, m], d,
        )

    def hot(k, half):
        rows = lax.broadcasted_iota(jnp.int32, (HALF * CAP, ROWS), 0) + half * (HALF * CAP)
        return jnp.where(rows == slots[k], 1.0, 0.0).astype(BF16)

    barrier = pltpu.get_barrier_semaphore()

    def greet(k):
        pl.semaphore_signal(barrier, inc=1, device_id=peer(k), device_id_type=MESH)

    slots[0] = slot_ref[...]
    loop(1, PEERS, greet)
    for step in (1, -1):
        pl.semaphore_signal(barrier, inc=1, device_id=along(step), device_id_type=MESH)
    pl.semaphore_wait(barrier, PEERS + 1)

    loop(1, MATES, lambda m: weight_copy(m).start())
    loop(1, PEERS, lambda k: slot_copy(k).start())

    def chip_at(core, i):
        return (i * (7 + 2 * core)) % CHIPS

    def send_step(t, i):
        m = chip_at(c, i)

        @pl.when(m > 0)
        def _():
            token_copy(t, 2 * m).start()

        token_copy(t, 2 * m + 1).start()

    def pair_at(i):
        return 2 * chip_at(c, i), 2 * chip_at(1 - c, i) + 1

    loop(0, WINDOW, lambda i: send_step(0, i))
    mine = [
        pltpu.make_async_copy(w_ref.at[:, :, columns(mate)], wbuf.at[z * MATES + mate], here.at[0])
    ] + [
        pltpu.make_async_copy(
            (x_ref, g_ref)[t].at[:, columns(y * MATES + mate)], recv.at[t, 0], here.at[1 + t]
        )
        for t in range(2)
    ]
    for copy in mine:
        copy.start()
    for copy in mine:
        copy.wait()

    loop(1, MATES, lambda m: weight_copy(m).wait_recv())
    weight_hop(0, 0).start()
    weight_hop(1, 0).start()
    loop(1, PEERS, lambda k: slot_copy(k).wait_recv())

    def rows_of(i):
        return pl.ds(pl.multiple_of(2 * CAP * i, 2 * CAP), 2 * CAP)

    def take_rows(t, i):
        ks = pair_at(i)

        @pl.when(i > 0)
        def _():
            token_copy(t, ks[0]).wait_recv()

        token_copy(t, ks[1]).wait_recv()
        for half in range(2):
            both = [
                jnp.dot(hot(k, half), recv[t, k], preferred_element_type=F32)
                .reshape(HALF, CAP, SLICE)
                for k in ks
            ]
            spread[t, half * HALF : (half + 1) * HALF, rows_of(i), :] = jnp.concatenate(
                both, axis=1
            ).astype(BF16)

    def to_rows(k, place):
        at = pl.ds(pl.multiple_of(CAP * place, CAP), CAP)
        lanes = packed[:, at, :].reshape(HALF * CAP, 2 * RANK).T
        high = lanes.astype(BF16)
        rest = (lanes - high.astype(F32)).astype(BF16)
        total = jnp.zeros((2 * RANK, ROWS), F32)
        for half in range(2):
            r = slice(half * RANK, (half + 1) * RANK)
            total += jnp.dot(
                jnp.concatenate([high[r], rest[r]], axis=0), hot(k, half), preferred_element_type=F32
            )
        part[k] = total[:RANK] + total[RANK:]

    def low_send(t, half):
        depth = PEERS * CAP // 2
        rows = slice(half * depth, (half + 1) * depth)

        def low_parts(p):
            packed[p, rows] = jnp.concatenate(
                [
                    lax.dot_general(spread[t, o, rows], wbuf[o, t], NT, preferred_element_type=F32)
                    for o in (p, p + HALF)
                ],
                axis=1,
            )

        def give(i):
            mine, theirs = pair_at(i)
            to_rows(theirs, 2 * i + 1)
            pair_copy(t, chip_at(1 - c, i)).start()
            to_rows(mine, 2 * i)

        def add(i):
            m = chip_at(c, i)
            pair_copy(t, m).wait_recv()
            pair[t, m] = pair[t, m] + part[2 * m]

            @pl.when(m > 0)
            def _():
                sum_copy(t, m).start()

        loop(0, HALF, low_parts)
        steps = half * CHIPS // 2, (half + 1) * CHIPS // 2
        loop(*steps, give)
        loop(*steps, add)

    def low_sum(t):
        loop(1, CHIPS, lambda m: sum_copy(t, m).wait_recv())
        total = pair[t, 0]
        for m in range(1, CHIPS):
            total += rsum[t, m]
        full[t, 0] = total.astype(BF16)
        low_pass(t, 0).start()
        loop(1, CHIPS, lambda i: low_copy(t, chip_at(c, i)).start())

    def low_spread(t):
        def hand_on(i):
            m = chip_at(c, i)
            low_copy(t, m).wait_recv()
            low_pass(t, m).start()

        def two(i):
            low_pass(t, chip_at(1 - c, i)).wait_recv()
            both = [
                jnp.concatenate(
                    [
                        lax.dot_general(hot(k, half), full[t, k], NT, preferred_element_type=F32)
                        for half in range(2)
                    ],
                    axis=1,
                ).reshape(HALF, CAP, 2 * RANK)
                for k in pair_at(i)
            ]
            low[t, :, rows_of(i), :] = jnp.concatenate(both, axis=1).astype(BF16)

        loop(1, CHIPS, hand_on)
        loop(0, CHIPS, two)

    def outer(t, plane, h, store):
        def one(i):
            o = plane * MATES + h * QUARTER + i
            p, half = o % HALF, o // HALF
            lhs = low[t, p].T
            lhs = jnp.where(half == 0, lhs[:RANK], lhs[RANK:])
            store(i, jnp.dot(lhs, spread[1 - t, o], preferred_element_type=F32))

        loop(0, QUARTER, one)

    def ring_step(t, h, arm, s):
        sign = (1 - 2 * arm) * (1 - 2 * h)
        hops = (UP, DOWN)[arm]
        place = arm * UP + s - 1
        if s > 0:
            ring_copy(t, h, arm, s - 1).wait_recv()

        def store(i, term):
            if s == 0:
                first[t, h, arm, 0, i] = term.astype(BF16)
            elif s == 1:
                ring[t, h, place, i] = first[t, h, arm, 1, i].astype(F32) + term
            else:
                ring[t, h, place, i] = ring[t, h, place, i] + term

        outer(t, (z - sign * (hops - s) + NZ) % NZ, h, store)
        ring_copy(t, h, arm, s).start()

    def ring_end(t):
        for h in range(2):
            ring_copy(t, h, 0, UP - 1).wait_recv()
            ring_copy(t, h, 1, DOWN - 1).wait_recv()

            def store(i, term, h=h):
                arrived = ring[t, h, UP - 1, i] + ring[t, h, UP + DOWN - 1, i]
                last[t, h * QUARTER + i] = term + arrived

            outer(t, z, h, store)

            def give(i, h=h):
                j = h * QUARTER + i
                m = (j // NC - x + NX) % NX * NC + (j % NC - c + NC) % NC

                @pl.when(m > 0)
                def _():
                    grad_copy(t, m).start()

            loop(0, QUARTER, give)
        out_ref[1 - t, :, columns(mate)] = last[t, mate]

    def ring_both(t, s):
        for arm in range(2 if s < DOWN else 1):
            for h in range(2):
                ring_step(t, h, arm, s)

    def paced(t, lo, hi, ahead):
        def step(i):
            n = i + ahead

            @pl.when(n < CHIPS)
            def _():
                send_step(t, n)

            if t == 0:

                @pl.when(n >= CHIPS)
                def _():
                    send_step(1, n - CHIPS)

            take_rows(t, i)

        loop(lo, hi, step)

    cuts = (0, *HOPS, CHIPS)
    for s in range(1, UP + 1):
        paced(0, cuts[s - 1], cuts[s], WINDOW)
        weight_wait(0, s - 1)
        if s < UP:
            weight_hop(0, s).start()
            weight_wait(1, s - 1)
        if s < DOWN:
            weight_hop(1, s).start()
    loop(WINDOW, WINDOW + EXTRA, lambda i: send_step(1, i))
    low_send(0, 0)
    low_send(0, 1)
    paced(1, 0, SUM_AT, WINDOW + EXTRA)
    low_sum(0)
    paced(1, SUM_AT, CHIPS // 2, WINDOW + EXTRA)
    loop(0, CHIPS, lambda m: pair_copy(0, m).wait_send())
    low_send(1, 0)
    paced(1, CHIPS // 2, SPREAD_AT, WINDOW + EXTRA)
    low_spread(0)
    paced(1, SPREAD_AT, CHIPS, WINDOW + EXTRA)
    ring_both(0, 0)
    low_send(1, 1)
    ring_both(0, 1)
    low_sum(1)
    ring_both(0, 2)
    low_spread(1)
    ring_both(1, 0)
    ring_both(0, 3)
    ring_both(1, 1)
    ring_end(0)
    ring_both(1, 2)
    ring_both(1, 3)
    ring_end(1)

    for t in range(2):
        loop(1, MATES, lambda m: grad_copy(t, m).wait())
        for arm, hops in enumerate((UP, DOWN)):
            for s in range(hops):
                for h in range(2):
                    ring_copy(t, h, arm, s).wait_send()
        loop(1, CHIPS, lambda m: low_copy(t, m).wait_send())
        loop(0, CHIPS, lambda m: low_pass(t, m).wait_send())
        loop(1, CHIPS, lambda m: sum_copy(t, m).wait_send())
        loop(1, PEERS, lambda k: token_copy(t, k).wait_send())
    loop(0, CHIPS, lambda m: pair_copy(1, m).wait_send())
    loop(1, PEERS, lambda k: slot_copy(k).wait_send())
    loop(1, MATES, lambda m: weight_copy(m).wait_send())
    for arm, hops in enumerate((UP, DOWN)):
        for s in range(hops):
            weight_hop(arm, s).wait_send()


def summed_grads(layer_input, output_grad, slot, weights):
    vmem = pl.BlockSpec(memory_space=pltpu.VMEM)
    hbm = pl.BlockSpec(memory_space=pl.ANY)
    sems = [
        (PEERS,), (PEERS,), (MATES,), (MATES,), (2, UP), (2, UP), (2, PEERS), (2, PEERS),
        (2, CHIPS), (2, CHIPS), (2, CHIPS), (2, CHIPS), (2, CHIPS), (2, CHIPS), (2, CHIPS), (2, CHIPS),
        (2, 2, UP + DOWN), (2, 2, UP + DOWN), (2, MATES), (2, MATES), (3,),
    ]
    return pl.pallas_call(
        kernel,
        out_shape=jax.ShapeDtypeStruct((2, RANK, MATES * SLICE), F32),
        in_specs=[hbm, hbm, vmem, vmem],
        out_specs=vmem,
        scratch_shapes=[
            pltpu.VMEM((PEERS, 1, ROWS), jnp.int32),
            pltpu.VMEM((OWNERS, 2, RANK, SLICE), BF16),
            pltpu.VMEM((2, PEERS, ROWS, SLICE), BF16),
            pltpu.VMEM((2, OWNERS, PEERS * CAP, SLICE), BF16),
            pltpu.VMEM((HALF, PEERS * CAP, 2 * RANK), F32),
            pltpu.VMEM((PEERS, RANK, ROWS), F32),
            pltpu.VMEM((2, CHIPS, RANK, ROWS), F32),
            pltpu.VMEM((2, CHIPS, RANK, ROWS), F32),
            pltpu.VMEM((2, PEERS, RANK, ROWS), BF16),
            pltpu.VMEM((2, HALF, PEERS * CAP, 2 * RANK), BF16),
            pltpu.VMEM((2, 2, 2, 2, QUARTER, RANK, SLICE), BF16),
            pltpu.VMEM((2, 2, UP + DOWN, QUARTER, RANK, SLICE), F32),
            pltpu.VMEM((2, MATES, RANK, SLICE), F32),
            *[pltpu.SemaphoreType.DMA(s) for s in sems],
        ],
        compiler_params=pltpu.CompilerParams(
            collective_id=0, has_side_effects=True, vmem_limit_bytes=62 << 20
        ),
        cost_estimate=pl.CostEstimate(flops=20 << 30, bytes_accessed=16 << 20, transcendentals=0),
    )(layer_input, output_grad, slot, weights)


def per_device(layer_input, output_grad, adapter_ids, owner_map, weights, moment, second):
    slot = slot_of_rows(adapter_ids, owner_map)[None, :]
    grads = ADAPTER_SCALING * summed_grads(layer_input, output_grad, slot, weights[0])
    return adam_step(grads[None], moment, second)


def solution(mesh):
    split = Mesh(np.asarray(mesh.devices).reshape(NY, NX, NZ, NC), ("y", "x", "z", "c"))
    ep = ("x", "z", "c")
    tokens = P(("y",) + ep, None)
    state = P(ep, None, None, "y")
    return jax.shard_map(
        per_device,
        mesh=split,
        in_specs=(tokens, tokens, tokens, P(), state, state, state),
        out_specs=(state, state, state),
        check_vma=False,
    )
```
